32 devices in a mesh: ctx: 4 (over z), head: 8 (over y, x, core).
Axes of the slice: x: 2, y: 2, z: 4, core: 2. Of those that a mesh axis runs over, the one named last changes fastest.
Arguments:
- queries: bfloat16 [8192, 4096], P(('ctx', 'head')), may hold values from -8 to 8
- keys: bfloat16 [8192, 2048], P(('ctx', 'head')), may hold values from -8 to 8
- values: bfloat16 [8192, 2048], P(('ctx', 'head')), may hold values from -18 to 18
- grad_out: bfloat16 [8192, 4096], P(('ctx', 'head')), may hold values from -18 to 18
Outputs:
- attended: bfloat16 [8192, 4096], P(('ctx', 'head'))
- grad_queries: bfloat16 [8192, 4096], P(('ctx', 'head'))
- grad_keys: bfloat16 [8192, 2048], P(('ctx', 'head'))
- grad_values: bfloat16 [8192, 2048], P(('ctx', 'head'))
The draws below stay inside these ranges and needn't reach their ends.
All inputs are finite; a program needn't handle non-finite values.
Results may differ from the reference program's by a relative error of at most 0.02.
Values may be sent and summed in bfloat16 or wider, within the bound.
A program may use at most 256 MiB of HBM per device.

```python
import jax
import jax.numpy as jnp
from jax import lax

HD = 128
QH = 32
KVH = 16
WIN = 1024
QPRE = 168
BLK = 256
SEQ = 8192


def draw_queries(key, part):
    base_rows = jnp.clip(2.0 * jax.random.normal(jax.random.fold_in(key, 3), (SEQ, QH, HD), jnp.float32), -8.0, 8.0)
    return base_rows.reshape(SEQ, QH * HD).astype(jnp.bfloat16)


def draw_keys(key, part):
    base_rows = jnp.clip(jax.random.normal(jax.random.fold_in(key, 4), (SEQ, KVH, HD), jnp.float32), -6.0, 6.0)
    return base_rows.reshape(SEQ, KVH * HD).astype(jnp.bfloat16)


def block_scale(rng, shape, pieces, smallest, high):
    loudness = 1.0
    for dim, parts in pieces:
        heights = jax.random.uniform(jax.random.fold_in(jax.random.fold_in(rng, 6), dim), (parts,), jnp.float32, smallest / len(pieces), high / len(pieces))
        loudness = loudness * jnp.repeat(jnp.exp(heights), shape[dim] // parts).reshape((-1,) + (1,) * (len(shape) - 1 - dim))
    return loudness


def normal_values(rng, extent, scale, bound, cuts=(), kind=jnp.bfloat16):
    values = scale * jax.random.normal(rng, extent, jnp.float32)
    if cuts:
        values = values * block_scale(rng, extent, cuts, -0.22, 0.18)
    return jnp.clip(values, -bound, bound).astype(kind)


def setup_inputs(seed: int = 0) -> dict:
    key_list = jax.random.split(jax.random.key(seed), 5)
    queries = draw_queries(jax.random.fold_in(key_list[4], 71), 0)
    keys = draw_keys(jax.random.fold_in(key_list[4], 71), 0)
    values = normal_values(key_list[2], (SEQ, KVH * HD), 3.0, 18.0, ((0, 32),))
    grad_out = normal_values(key_list[3], (SEQ, QH * HD), 3.0, 18.0, ((0, 32),))
    return {"queries": queries, "keys": keys, "values": values, "grad_out": grad_out}


def arrange(block, shared_heads, group_size):
    rows = block.shape[0]
    width = block.shape[2]
    stacked = block.reshape(rows, shared_heads, group_size, width)
    return jnp.transpose(stacked, (1, 2, 0, 3)).reshape(shared_heads, group_size * rows, width)


def restore(stack, rows, group_size):
    shared_heads = stack.shape[0]
    width = stack.shape[2]
    split = stack.reshape(shared_heads, group_size, rows, width)
    return jnp.transpose(split, (2, 0, 1, 3)).reshape(rows, shared_heads * group_size, width)


def attend(queries, keys_ext, values_ext, grads, first_query):
    query_count = queries.shape[0]
    query_heads = queries.shape[1]
    shared_heads = keys_ext.shape[1]
    head_width = queries.shape[2]
    group_size = query_heads // shared_heads
    block_rows = min(BLK, query_count)
    key_span = WIN + block_rows
    block_total = query_count // block_rows
    scale = QPRE ** -0.5

    def block_step(totals, block):
        key_total, value_total = totals
        first_row = block * block_rows
        query_block = lax.dynamic_slice_in_dim(queries, first_row, block_rows, 0)
        grad_block = lax.dynamic_slice_in_dim(grads, first_row, block_rows, 0)
        key_block = lax.dynamic_slice_in_dim(keys_ext, first_row, key_span, 0)
        value_block = lax.dynamic_slice_in_dim(values_ext, first_row, key_span, 0)
        query_pos = first_query + first_row + jnp.arange(block_rows, dtype=jnp.int32)
        key_pos = first_query - WIN + first_row + jnp.arange(key_span, dtype=jnp.int32)
        distance = query_pos[:, None] - key_pos[None, :]
        allowed = (distance >= 0) & (distance < WIN) & (key_pos[None, :] >= 0)
        allowed = jnp.tile(allowed, (group_size, 1))
        query_stack = arrange(query_block, shared_heads, group_size).astype(jnp.float32)
        grad_stack = arrange(grad_block, shared_heads, group_size).astype(jnp.float32)
        key_stack = jnp.transpose(key_block, (1, 0, 2)).astype(jnp.float32)
        value_stack = jnp.transpose(value_block, (1, 0, 2)).astype(jnp.float32)
        scores = jnp.einsum("hqd,hkd->hqk", query_stack, key_stack) * scale
        scores = jnp.where(allowed[None], scores, -jnp.inf)
        largest = jnp.max(scores, axis=-1, keepdims=True)
        unnormed = jnp.exp(scores - largest)
        probs = unnormed / jnp.sum(unnormed, axis=-1, keepdims=True)
        probs_low = probs.astype(jnp.bfloat16)
        output_stack = jnp.einsum("hqk,hkd->hqd", probs_low.astype(jnp.float32), value_stack).astype(jnp.bfloat16)
        grad_probs = jnp.einsum("hqd,hkd->hqk", grad_stack, value_stack)
        inner = jnp.sum(grad_stack * output_stack.astype(jnp.float32), axis=-1, keepdims=True)
        grad_scores = (probs * (grad_probs - inner) * scale).astype(jnp.bfloat16)
        grad_query = jnp.einsum("hqk,hkd->hqd", grad_scores.astype(jnp.float32), key_stack).astype(jnp.bfloat16)
        grad_key = jnp.einsum("hqk,hqd->khd", grad_scores.astype(jnp.float32), query_stack)
        grad_value = jnp.einsum("hqk,hqd->khd", probs_low.astype(jnp.float32), grad_stack)
        key_old = lax.dynamic_slice_in_dim(key_total, first_row, key_span, 0)
        value_old = lax.dynamic_slice_in_dim(value_total, first_row, key_span, 0)
        key_total = lax.dynamic_update_slice_in_dim(key_total, key_old + grad_key, first_row, 0)
        value_total = lax.dynamic_update_slice_in_dim(value_total, value_old + grad_value, first_row, 0)
        return (key_total, value_total), (restore(output_stack, block_rows, group_size), restore(grad_query, block_rows, group_size))

    zeros_ext = jnp.zeros((WIN + query_count, shared_heads, head_width), jnp.float32)
    (key_total, value_total), (outputs, grad_queries) = lax.scan(block_step, (zeros_ext, zeros_ext), jnp.arange(block_total, dtype=jnp.int32))
    attended = outputs.reshape(query_count, query_heads, head_width)
    grad_queries = grad_queries.reshape(query_count, query_heads, head_width)
    return attended, grad_queries, key_total, value_total


def reference(queries, keys, values, grad_out):
    query_rows = queries.reshape(SEQ, QH, HD)
    key_rows = keys.reshape(SEQ, KVH, HD)
    value_rows = values.reshape(SEQ, KVH, HD)
    grad_rows = grad_out.reshape(SEQ, QH, HD)
    padding = jnp.zeros((WIN, KVH, HD), keys.dtype)
    keys_ext = jnp.concatenate([padding, key_rows], axis=0)
    values_ext = jnp.concatenate([padding, value_rows], axis=0)
    attended, grad_queries, key_total, value_total = attend(query_rows, keys_ext, values_ext, grad_rows, 0)
    grad_keys = key_total[WIN:].astype(jnp.bfloat16)
    grad_values = value_total[WIN:].astype(jnp.bfloat16)
    return (attended.reshape(SEQ, QH * HD), grad_queries.reshape(SEQ, QH * HD), grad_keys.reshape(SEQ, KVH * HD), grad_values.reshape(SEQ, KVH * HD))
```

```python
import functools

import jax
import jax.numpy as jnp
from jax import lax
from jax.experimental import pallas as pl
from jax.experimental.pallas import tpu as pltpu
from jax.sharding import PartitionSpec as P

HD = 128
WIN = 1024
QPRE = 168
SCALE = QPRE ** -0.5
LOG2E = 1.4426950408889634
FAR = 1e30
MESH = pl.DeviceIdType.MESH


def contract(a, b):
    return jnp.dot(a, b, preferred_element_type=jnp.float32)


def kernel(
    chips, head_size,
    q_in, k_in, v_in, g_in, o_out, dq_out, dk_out, dv_out,
    qg, kv, obuf, dqbuf, part, relay, back, own, final,
    qg_sem, kv_sem, relay_sem, back_sem, out_recv, out_local,
    near_send, one_send, two_send, fwd_send, part_send, out_send,
):
    rows = q_in.shape[0]
    heads = qg.shape[0]
    width = qg.shape[4]
    linear = lax.axis_index("ctx") * head_size + lax.axis_index("head")
    chip = linear // 2
    core = linear % 2
    other = 1 - core
    odd = chip % 2
    has_one = chip >= 1
    has_two = chip >= 2
    to_one = chip + 1 < chips
    to_two = chip + 2 < chips

    def device(c, k):
        index = c * 2 + k
        return (index // head_size, index % head_size)

    def remote(src, dst, send, recv, c, k):
        return pltpu.make_async_remote_copy(
            src_ref=src, dst_ref=dst, send_sem=send, recv_sem=recv,
            device_id=device(c, k), device_id_type=MESH,
        )

    def drain(ref, sem):
        pltpu.make_async_copy(ref, ref, sem).wait()

    barrier = pltpu.get_barrier_semaphore()
    pl.semaphore_signal(barrier, inc=1, device_id=device(chip, other), device_id_type=MESH)
    for step, there in ((-2, has_two), (-1, has_one), (1, to_one), (2, to_two)):
        @pl.when(there)
        def _():
            for k in (0, 1):
                pl.semaphore_signal(barrier, inc=1, device_id=device(chip + step, k), device_id_type=MESH)
    greeted = (1 + 2 * jnp.minimum(chip, 2) + 2 * jnp.minimum(chips - 1 - chip, 2)).astype(jnp.int32)
    pl.semaphore_wait(barrier, greeted)

    def send_head(h, carry):
        for half in (0, 1):
            column = half * heads + h
            narrow = pl.ds(pl.multiple_of(column * HD, HD), HD)
            wide = pl.ds(pl.multiple_of(column * width, width), width)
            pairs = [(ref.at[:, narrow], i) for i, ref in enumerate((k_in, v_in))]
            wides = [(ref.at[:, wide], i) for i, ref in enumerate((q_in, g_in))]

            @pl.when(to_two)
            def _():
                for src, i in pairs:
                    remote(src, kv.at[h, i, core], two_send, kv_sem.at[h, 0], chip + 2, half).start()

            @pl.when(to_one & (odd == 0))
            def _():
                for src, i in pairs:
                    remote(src, kv.at[h, i, 2 + core], one_send, kv_sem.at[h, 1], chip + 1, half).start()

            @pl.when(core == half)
            def _():
                for src, i in pairs:
                    pltpu.make_async_copy(src, kv.at[h, i, 4 + core], kv_sem.at[h, 2]).start()
                for src, i in wides:
                    pltpu.make_async_copy(src, qg.at[h, i, core], qg_sem.at[h]).start()

            @pl.when(core != half)
            def _():
                for src, i in pairs:
                    remote(src, kv.at[h, i, 4 + core], near_send.at[0], kv_sem.at[h, 2], chip, half).start()
                for src, i in wides:
                    remote(src, qg.at[h, i, core], near_send.at[1], qg_sem.at[h], chip, half).start()
        return carry

    lax.fori_loop(0, heads, send_head, 0)

    for slot, there in ((0, has_two), (1, has_one)):
        @pl.when(jnp.logical_not(there))
        def _():
            for i in (0, 1):
                for b in (0, 1):
                    kv[:, i, 2 * slot + b] = jnp.zeros((heads, rows, HD), jnp.bfloat16)

    sub = lax.broadcasted_iota(jnp.int32, (rows, 2 * rows), 0)
    lane = lax.broadcasted_iota(jnp.int32, (rows, 2 * rows), 1)
    early = sub > jnp.where(lane >= rows, lane - rows, lane)
    valid = {0: has_two, 1: has_one}
    far_bias = jnp.where(has_two, 0.0, -FAR)

    def compute(h):
        grads = {}
        for t in (0, 1):
            q2, g2 = qg[h, 0, t], qg[h, 1, t]
            qt = jnp.concatenate([q2[:, :HD].T, q2[:, HD:].T], axis=1)
            gt = jnp.concatenate([g2[:, :HD].T, g2[:, HD:].T], axis=1)
            keys = [kv[h, 0, t + b] for b in range(5)]
            vals = [kv[h, 1, t + b] for b in range(5)]
            raw = [contract(k, qt) for k in keys]
            scores = [jnp.where(early, raw[0] + far_bias, raw[4])] + raw[1:4]
            slots = [2] + [(t + b) // 2 for b in (1, 2, 3)]
            tops = []
            for s, slot in zip(scores, slots):
                top = jnp.max(s, axis=0, keepdims=True)
                tops.append(jnp.where(valid[slot], top, -FAR) if slot < 2 else top)
            top = functools.reduce(jnp.maximum, tops) * (SCALE * LOG2E)
            probs, total = [], None
            for s, slot in zip(scores, slots):
                less = jnp.where(valid[slot], top, FAR) if slot < 2 else top
                p = jnp.exp2(s * (SCALE * LOG2E) - less)
                summed = jnp.sum(p, axis=0, keepdims=True)
                total = summed if total is None else total + summed
                probs.append(p.astype(jnp.bfloat16))
            inverse = 1.0 / total
            nothing = jnp.zeros_like(probs[0])

            def spread(items):
                return [jnp.where(early, items[0], nothing)] + items[1:] + [jnp.where(early, nothing, items[0])]

            low = spread(probs)
            out = functools.reduce(jnp.add, [contract(v.T, p) for v, p in zip(vals, low)]) * inverse
            out_low = out.astype(jnp.bfloat16)
            grad = gt.astype(jnp.float32)
            inner = jnp.sum(grad * out_low.astype(jnp.float32), axis=0, keepdims=True)
            dp = [contract(v, gt) for v in vals]
            dp = [jnp.where(early, dp[0], dp[4])] + dp[1:4]
            ds = spread([(p.astype(jnp.float32) * (d - inner)).astype(jnp.bfloat16) for p, d in zip(probs, dp)])
            dq = functools.reduce(jnp.add, [contract(k.T, d) for k, d in zip(keys, ds)]) * (inverse * SCALE)
            dq_low = dq.astype(jnp.bfloat16)
            for i in (0, 1):
                lanes = slice(i * rows, (i + 1) * rows)
                obuf[h, t, :, i * HD:(i + 1) * HD] = out_low[:, lanes].T
                dqbuf[h, t, :, i * HD:(i + 1) * HD] = dq_low[:, lanes].T
            gn = (grad * inverse).astype(jnp.bfloat16).T
            qn = (qt.astype(jnp.float32) * (inverse * SCALE)).astype(jnp.bfloat16).T
            for b in range(5):
                for i, term in ((0, contract(ds[b], qn)), (1, contract(low[b], gn))):
                    place = (i, t + b)
                    grads[place] = term if place not in grads else grads[place] + term
        for i in (0, 1):
            for b in range(4):
                part[h, b // 2, i, b % 2] = grads[i, b].astype(jnp.bfloat16)
            for b in (4, 5):
                own[h, i, b - 4] = grads[i, b]

    def hand_out(src, out, column, columns, number):
        cols = pl.ds(pl.multiple_of(column * columns, columns), columns)
        for t in (0, 1):
            @pl.when(core == t)
            def _():
                pltpu.make_async_copy(src.at[t], out.at[:, cols], out_local.at[number]).start()

            @pl.when(core != t)
            def _():
                remote(src.at[t], out.at[:, cols], out_send.at[number], out_recv.at[number], chip, t).start()

    def merge(h):
        @pl.when((odd == 1) & has_two)
        def _():
            drain(relay.at[h], relay_sem.at[h])
            part[h, 0] = (part[h, 0].astype(jnp.float32) + relay[h].astype(jnp.float32)).astype(jnp.bfloat16)
            remote(part.at[h, 0], back.at[h, 0], part_send.at[h, 0], back_sem.at[h, 0], chip - 2, core).start()

    def step(h, carry):
        drain(kv.at[h, :, 4:6], kv_sem.at[h, 2])
        drain(qg.at[h], qg_sem.at[h])

        @pl.when(has_two)
        def _():
            drain(kv.at[h, :, 0:2], kv_sem.at[h, 0])

        @pl.when((odd == 1) & has_two)
        def _():
            remote(kv.at[h, :, 0:2], kv.at[h, :, 2:4], fwd_send.at[h], kv_sem.at[h, 1], chip - 1, core).start()

        @pl.when(has_one)
        def _():
            drain(kv.at[h, :, 2:4], kv_sem.at[h, 1])

        compute(h)

        @pl.when((odd == 0) & has_two)
        def _():
            remote(part.at[h, 1], relay.at[h], part_send.at[h, 1], relay_sem.at[h], chip + 1, core).start()
            remote(part.at[h, 0], back.at[h, 0], part_send.at[h, 0], back_sem.at[h, 0], chip - 2, core).start()

        @pl.when(odd == 1)
        def _():
            remote(part.at[h, 1], back.at[h, 1], part_send.at[h, 1], back_sem.at[h, 1], chip - 1, core).start()

        @pl.when(h >= 1)
        def _():
            merge(jnp.maximum(h - 1, 0))

        column = core * heads + h
        hand_out(obuf.at[h], o_out, column, width, 0)
        hand_out(dqbuf.at[h], dq_out, column, width, 1)
        return carry

    lax.fori_loop(0, heads, step, 0)
    merge(heads - 1)

    def finish(h, carry):
        @pl.when(to_two)
        def _():
            drain(back.at[h, 0], back_sem.at[h, 0])
            own[h] = own[h] + back[h, 0].astype(jnp.float32)

        @pl.when(odd == 0)
        def _():
            drain(back.at[h, 1], back_sem.at[h, 1])
            own[h] = own[h] + back[h, 1].astype(jnp.float32)

        final[h] = own[h].astype(jnp.bfloat16)
        column = core * heads + h
        hand_out(final.at[h, 0], dk_out, column, HD, 2)
        hand_out(final.at[h, 1], dv_out, column, HD, 3)
        return carry

    lax.fori_loop(0, heads, finish, 0)

    half_kv = k_in.shape[1] // 2
    half_q = q_in.shape[1] // 2
    for number, ref, size in ((0, o_out, half_q), (1, dq_out, half_q), (2, dk_out, half_kv), (3, dv_out, half_kv)):
        for sems in (out_local, out_send, out_recv):
            drain(ref.at[:, 0:size], sems.at[number])
    drain(k_in, near_send.at[0])
    drain(q_in, near_send.at[1])

    @pl.when(to_two)
    def _():
        drain(k_in, two_send)
        drain(v_in, two_send)

    @pl.when(to_one & (odd == 0))
    def _():
        drain(k_in, one_send)
        drain(v_in, one_send)

    def sent(h, carry):
        @pl.when(has_two)
        def _():
            drain(part.at[h, 0], part_send.at[h, 0])

        @pl.when((odd == 1) | has_two)
        def _():
            drain(part.at[h, 1], part_send.at[h, 1])

        @pl.when((odd == 1) & has_two)
        def _():
            drain(kv.at[h, :, 0:2], fwd_send.at[h])
        return carry

    lax.fori_loop(0, heads, sent, 0)


def body(head_size, chips, queries, keys, values, grad_out):
    rows = queries.shape[0]
    heads = keys.shape[1] // HD // 2
    width = queries.shape[1] // (2 * heads)
    assert rows * 4 == WIN and width == 2 * HD
    low, full = jnp.bfloat16, jnp.float32
    dma = pltpu.SemaphoreType.DMA
    anywhere = pl.BlockSpec(memory_space=pl.ANY)
    flops = 12 * rows * (queries.shape[1] // HD) * (WIN + rows) * HD
    return pl.pallas_call(
        functools.partial(kernel, chips, head_size),
        out_shape=tuple(jax.ShapeDtypeStruct(a.shape, low) for a in (queries, queries, keys, keys)),
        in_specs=[anywhere] * 4,
        out_specs=(anywhere,) * 4,
        scratch_shapes=[
            pltpu.VMEM((heads, 2, 2, rows, width), low),
            pltpu.VMEM((heads, 2, 6, rows, HD), low),
            pltpu.VMEM((heads, 2, rows, width), low),
            pltpu.VMEM((heads, 2, rows, width), low),
            pltpu.VMEM((heads, 2, 2, 2, rows, HD), low),
            pltpu.VMEM((heads, 2, 2, rows, HD), low),
            pltpu.VMEM((heads, 2, 2, 2, rows, HD), low),
            pltpu.VMEM((heads, 2, 2, rows, HD), full),
            pltpu.VMEM((heads, 2, 2, rows, HD), low),
            dma((heads,)), dma((heads, 3)), dma((heads,)), dma((heads, 2)), dma((4,)), dma((4,)),
            dma((2,)), dma(()), dma(()), dma((heads,)), dma((heads, 2)), dma((4,)),
        ],
        cost_estimate=pl.CostEstimate(flops=flops, bytes_accessed=12 * 2 ** 20, transcendentals=flops // 1536),
        compiler_params=pltpu.CompilerParams(
            collective_id=0, has_side_effects=True, vmem_limit_bytes=56 * 2 ** 20
        ),
    )(queries, keys, values, grad_out)


def solution(mesh):
    head_size = mesh.shape["head"]
    chips = mesh.shape["ctx"] * head_size // 2
    placed = (P(("ctx", "head"), None),) * 4
    return jax.shard_map(
        functools.partial(body, head_size, chips), mesh=mesh, in_specs=placed, out_specs=placed, check_vma=False
    )
```
